512 devices in a mesh: au: 16 (over x_hi, y, core), vert: 32 (over z, x_lo).
Axes of the slice: x: 4 (x_hi: 2, x_lo: 2; x = x_hi * 2 + x_lo), y: 4, z: 16, core: 2. Of those that a mesh axis runs over, the one named last changes fastest.
Arguments:
- views: bfloat16 [32, 16, 16, 4096], P('vert', 'au'), may hold values from -6 to 6
- shifts: int32 [32, 16, 32], P('vert', 'au'), may hold values from -16 to 16
Outputs:
- refined: float32 [32, 16, 16, 4096], P('vert', None, 'au')
The draws below stay inside these ranges and needn't reach their ends.
All inputs are finite; a program needn't handle non-finite values.
Results may differ from the reference program's by a relative error of at most 0.0003.
Values may be sent and summed in bfloat16 or wider, within the bound.
A program may use at most 64 MiB of HBM per device.

```python
import jax
import jax.numpy as jnp
from jax import lax

ROWS_DEV = 16
W = 4096
L = 32
MAXS = 16
RAD = 2
N_AU = 16
N_VERT = 32


def draw_views(key, part):
    key = jax.random.fold_in(key, 11)
    first = jax.random.fold_in(key, 0)
    shape = (N_VERT, N_AU, ROWS_DEV, W)
    values = jax.random.truncated_normal(first, -6.0, 6.0, shape, jnp.float32)
    return values.astype(jnp.bfloat16)


def touch_ends(values, own_key, smallest, high):
    dims = values.shape
    index_at = [jax.random.randint(jax.random.fold_in(own_key, axis), (), 0, dims[axis]) for axis in range(len(dims))]
    values = values.at[tuple(index_at)].set(smallest)
    longest = dims.index(max(dims))
    index_at[longest] = (index_at[longest] + 1) % dims[longest]
    return values.at[tuple(index_at)].set(high)


def setup_inputs(seed: int = 0) -> dict:
    splits = jax.random.split(jax.random.key(seed), 3)
    return {
        "views": draw_views(jax.random.fold_in(splits[2], 71), 0),
        "shifts": touch_ends(jax.random.randint(splits[1], (N_VERT, N_AU, L), -MAXS, MAXS + 1), jax.random.fold_in(splits[1], 1), -MAXS, MAXS).astype(jnp.int32),
    }


def label_costs(band, mirror, shift_row):
    width = band.shape[1]
    own = jnp.pad(band.astype(jnp.float32), ((0, 0), (MAXS, MAXS)))
    other = jnp.pad(mirror.astype(jnp.float32), ((0, 0), (MAXS, MAXS)))

    def one_label(shift):
        moved = lax.dynamic_slice_in_dim(own, (MAXS + shift).astype(jnp.int32), width, 1)
        facing = lax.dynamic_slice_in_dim(other, (MAXS - shift).astype(jnp.int32), width, 1)
        return (moved - facing) ** 2

    squares = jax.vmap(one_label)(shift_row)
    padded = jnp.pad(squares, ((0, 0), (0, 0), (RAD, RAD)))
    total = padded[:, :, 0:width]
    for offset in range(1, 2 * RAD + 1):
        total = total + padded[:, :, offset:offset + width]
    return total


def soft_depth(cost, label_axis):
    scores = -0.5 * cost
    weight = jax.nn.softmax(scores, axis=label_axis)
    count = cost.shape[label_axis]
    shape = [1] * cost.ndim
    shape[label_axis] = count
    labels = jnp.arange(count, dtype=jnp.float32).reshape(shape)
    depth = jnp.sum(weight * labels, axis=label_axis)
    confidence = jnp.max(weight, axis=label_axis)
    return depth, confidence


def refine_epi(intens, depth, confidence):
    cams, rows, width = intens.shape
    padx = jnp.pad(intens, ((0, 0), (0, 0), (1, 1)))
    grad_x = 0.5 * (padx[:, :, 2:] - padx[:, :, :-2])
    padu = jnp.pad(intens, ((1, 1), (0, 0), (0, 0)))
    grad_u = 0.5 * (padu[2:] - padu[:-2])

    def boxed(field):
        padded = jnp.pad(field, ((1, 1), (0, 0), (RAD, RAD)))
        total = jnp.zeros((cams, rows, width), jnp.float32)
        for du in range(3):
            for dx in range(2 * RAD + 1):
                total = total + padded[du:du + cams, :, dx:dx + width]
        return total

    jxx = boxed(grad_x * grad_x)
    jxu = boxed(grad_x * grad_u)
    slope = -jxu / (jxx + 1.0)
    coherence = jxx / (jxx + 1.0)
    return (confidence * depth + 4.0 * coherence * slope) / (confidence + coherence)


def reference(views, shifts):
    slots, cams, rows, width = views.shape
    mirror = views.reshape(slots // 2, 2, cams, rows, width)[::-1, :, ::-1].reshape(slots, cams, rows, width)

    def per_view(items):
        band, facing, shift_row = items
        return soft_depth(label_costs(band, facing, shift_row), 0)

    depth, confidence = lax.map(per_view, (views.reshape(slots * cams, rows, width), mirror.reshape(slots * cams, rows, width), shifts.reshape(slots * cams, -1)))
    depth = depth.reshape(slots, cams, rows, width)
    confidence = confidence.reshape(slots, cams, rows, width)

    def per_slot(items):
        band, dmap, cmap = items
        return refine_epi(band.astype(jnp.float32), dmap, cmap)

    return lax.map(per_slot, (views, depth, confidence))
```

```python
import functools
import math

import jax
import jax.numpy as jnp
from jax import lax
from jax.experimental import pallas as pl
from jax.experimental.pallas import tpu as pltpu
from jax.sharding import PartitionSpec as P

MAXS = 16
RAD = 2
OFFS = 2 * MAXS + 1
CAMS = 16
ROWS = 16
TILES = 32
LANES = 128
SEG = 64
HALO = MAXS + RAD
EXT = SEG + 2 * HALO
BLOCK = 8
SCALE = math.sqrt(0.5 * math.log2(math.e))
FAR = 1e30
MESH = pl.DeviceIdType.MESH


def exchange_kernel(views, shifts, own, mir, band, flat, rows, shift_row, load_sem, zsend, zrecv, psend, precv, ready, go):
    au = lax.axis_index("au")
    vert = lax.axis_index("vert")
    facing = 30 - 2 * (vert // 2) + lax.rem(vert, 2)
    first = vert < 16

    load = pltpu.make_async_copy(views.at[0, 0], band, load_sem.at[0])
    load.start()
    load_shift = pltpu.make_async_copy(shifts.at[0], shift_row, load_sem.at[1])
    load_shift.start()

    def peer(k):
        return lax.rem(au + k, CAMS)

    def signal(sem, column, slot):
        pl.semaphore_signal(sem, inc=1, device_id={"au": column, "vert": slot}, device_id_type=MESH)

    barrier = pltpu.get_barrier_semaphore()

    @pl.when(first)
    def _():
        for k in range(CAMS):
            signal(barrier, peer(k), facing)
        for k in range(1, CAMS):
            signal(barrier, peer(k), vert)

    load.wait()
    for t in range(TILES):
        flat[pl.ds(t, ROWS, stride=TILES), :] = band[:, t * LANES : (t + 1) * LANES].astype(jnp.float32)
    for y in range(ROWS):
        rows[y, 0:TILES, :] = flat[y * TILES : (y + 1) * TILES, :].astype(jnp.bfloat16)
    load_shift.wait()
    labels = jnp.concatenate([shift_row[...].astype(jnp.float32), jnp.zeros((1, LANES - 32), jnp.float32)], axis=1)
    labels = jnp.broadcast_to(labels, (16, LANES)).astype(jnp.bfloat16)
    for y in range(ROWS):
        rows[y, TILES : TILES + 16, :] = labels

    across = [
        pltpu.make_async_remote_copy(
            src_ref=rows.at[peer(k), pl.ds(0, TILES)],
            dst_ref=mir.at[CAMS - 1 - au],
            send_sem=zsend.at[k],
            recv_sem=zrecv.at[k],
            device_id={"au": peer(k), "vert": facing},
            device_id_type=MESH,
        )
        for k in range(CAMS)
    ]
    inside = [
        pltpu.make_async_remote_copy(
            src_ref=rows.at[peer(k)],
            dst_ref=own.at[au],
            send_sem=psend.at[k],
            recv_sem=precv.at[k],
            device_id={"au": peer(k), "vert": vert},
            device_id_type=MESH,
        )
        for k in range(1, CAMS)
    ]
    keep = pltpu.make_async_copy(rows.at[au], own.at[au], load_sem.at[2])
    keep.start()

    @pl.when(first)
    def _():
        pl.semaphore_wait(barrier, CAMS - 1)
        for copy in inside:
            copy.start()
        pl.semaphore_wait(ready, CAMS)
        signal(go, au, facing)
        for copy in across:
            copy.start()

    @pl.when(jnp.logical_not(first))
    def _():
        pl.semaphore_wait(barrier, CAMS)
        for copy in across:
            copy.start()
        for k in range(CAMS):
            signal(ready, peer(k), facing)
        pl.semaphore_wait(go, 1)
        for copy in inside:
            copy.start()

    keep.wait()
    for copy in inside + across:
        copy.wait()


def exchange(views, shifts):
    return pl.pallas_call(
        exchange_kernel,
        out_shape=(
            jax.ShapeDtypeStruct((CAMS, TILES + 16, LANES), jnp.bfloat16),
            jax.ShapeDtypeStruct((CAMS, TILES, LANES), jnp.bfloat16),
        ),
        in_specs=[pl.BlockSpec(memory_space=pl.ANY)] * 2,
        out_specs=[pl.BlockSpec(memory_space=pl.ANY)] * 2,
        scratch_shapes=[
            pltpu.VMEM((ROWS, TILES * LANES), jnp.bfloat16),
            pltpu.VMEM((ROWS * TILES, LANES), jnp.float32),
            pltpu.VMEM((ROWS, TILES + 16, LANES), jnp.bfloat16),
            pltpu.VMEM((1, 32), jnp.int32),
            pltpu.SemaphoreType.DMA((3,)),
            pltpu.SemaphoreType.DMA((CAMS,)),
            pltpu.SemaphoreType.DMA((CAMS,)),
            pltpu.SemaphoreType.DMA((CAMS,)),
            pltpu.SemaphoreType.DMA((CAMS,)),
            pltpu.SemaphoreType.REGULAR,
            pltpu.SemaphoreType.REGULAR,
        ],
        compiler_params=pltpu.CompilerParams(collective_id=0, has_side_effects=True),
        name="exchange",
    )(views, shifts)


def spread(block, ref, first_row):
    for group in range(4):
        turned = block(group).T
        for half in range(2):
            ref[pl.ds(first_row * 8 + half * 4 + group, SEG, stride=8), :] = turned[half * SEG : (half + 1) * SEG]


def refine_kernel(own, mir, out, ext, facing, table, depths, costs, coh_ref, pull_ref):
    lane = lax.broadcasted_iota(jnp.int32, (8, LANES), 1)
    sub = lax.broadcasted_iota(jnp.int32, (8, LANES), 0)
    tile, member = lane % 32, lane // 32
    upper, group = sub >= 4, sub % 4
    zero = jnp.zeros((8, LANES), jnp.float32)

    def row(ref, i):
        if isinstance(i, int):
            return ref[i * 8 : i * 8 + 8, :]
        return ref[pl.ds(pl.multiple_of(i * 8, 8), 8), :]

    def put(ref, i, value):
        if isinstance(i, int):
            ref[i * 8 : i * 8 + 8, :] = value
        else:
            ref[pl.ds(pl.multiple_of(i * 8, 8), 8), :] = value

    def flat(ref, g):
        return ref[4 * g : 4 * g + 4, 0:TILES, :].astype(jnp.float32).reshape(LANES, LANES) * SCALE

    last_tile, first_tile = tile == TILES - 1, tile == 0
    for source, ref in ((own, ext), (mir, facing)):
        spread(functools.partial(flat, source), ref, HALO)
        for j in range(HALO):
            turned = pltpu.roll(row(ref, HALO + j), 4, 0)
            moved = jnp.where(last_tile, zero, pltpu.roll(turned, LANES - 1, 1))
            put(ref, HALO + SEG + j, jnp.where(upper, moved, turned))
            turned = pltpu.roll(row(ref, SEG + j), 4, 0)
            moved = jnp.where(first_tile, zero, pltpu.roll(turned, 1, 1))
            put(ref, j, jnp.where(upper, turned, moved))

    shift = own[:, TILES, :].astype(jnp.float32)
    offset = lax.broadcasted_iota(jnp.int32, (CAMS, LANES), 1).astype(jnp.float32) - MAXS
    often = jnp.zeros((CAMS, LANES), jnp.float32)
    total = jnp.zeros((CAMS, LANES), jnp.float32)
    for label in range(32):
        hit = shift[:, label : label + 1] == offset
        often = often + jnp.where(hit, 1.0, 0.0)
        total = total + jnp.where(hit, float(label), 0.0)
    both = often + pltpu.roll(total, 64, 1)

    def cams(g):
        return jnp.broadcast_to(both[4 * g : 4 * g + 4, None, :], (4, TILES, LANES)).reshape(LANES, LANES)

    for g in range(4):
        turned = cams(g).T
        for half in range(2):
            table[pl.ds(half * 4 + g, LANES, stride=8), :] = turned

    def after(value):
        a = pltpu.roll(value, LANES - 32, 1)
        b = jnp.where(group < 3, pltpu.roll(a, 7, 0), zero)
        return jnp.where(member < 3, a, b)

    def before(value):
        a = pltpu.roll(value, 32, 1)
        b = jnp.where(group > 0, pltpu.roll(a, 1, 0), zero)
        return jnp.where(member > 0, a, b)

    def boxed(values):
        pairs = [values[i] + values[i + 1] for i in range(len(values) - 1)]
        return [pairs[i] + pairs[i + 2] + values[i + 4] for i in range(len(values) - 4)]

    outside_left = jnp.logical_and(first_tile, jnp.logical_not(upper))
    outside_right = jnp.logical_and(last_tile, upper)

    def block(b, _):
        start = b * BLOCK
        left = jnp.where(jnp.logical_and(outside_left, b == 0), zero, zero + 1.0)
        right = jnp.where(jnp.logical_and(outside_right, b == SEG // BLOCK - 1), zero, zero + 1.0)

        def inside(values):
            return [v * left for v in values[:RAD]] + values[RAD:-RAD] + [v * right for v in values[-RAD:]]

        base = start + HALO - RAD
        width = BLOCK + 2 * RAD
        gx = inside([row(ext, base + i + 1) - row(ext, base + i - 1) for i in range(width)])
        gu = [after(row(ext, base + i)) - before(row(ext, base + i)) for i in range(width)]
        xx = boxed([g * g for g in gx])
        xu = boxed([g * h for g, h in zip(gx, gu)])
        unit = 0.25 / (SCALE * SCALE)
        cohs, pulls = [], []
        for i in range(BLOCK):
            jxx = (xx[i] + after(xx[i]) + before(xx[i])) * unit
            jxu = (xu[i] + after(xu[i]) + before(xu[i])) * unit
            inv = 1.0 / (jxx + 1.0)
            coh = jxx * inv
            put(coh_ref, i, coh)
            put(pull_ref, i, 4.0 * coh * (-jxu * inv))

        best = [zero + FAR for _ in range(BLOCK)]
        for s in range(OFFS):
            step = s - MAXS
            squares = []
            for i in range(width):
                d = row(ext, base + i + step) - row(facing, base + i - step)
                squares.append(d * d)
            miss = jnp.where(row(table, s) > 0.0, 0.0, FAR)
            for i, cost in enumerate(boxed(inside(squares))):
                cost = cost + miss
                put(costs, s * BLOCK + i, cost)
                best[i] = jnp.minimum(best[i], cost)
        den = [zero for _ in range(BLOCK)]
        num = [zero for _ in range(BLOCK)]
        for s in range(OFFS):
            n, m = row(table, s), row(table, 64 + s)
            for i in range(BLOCK):
                e = jnp.exp2(best[i] - row(costs, s * BLOCK + i))
                den[i] = den[i] + e * n
                num[i] = num[i] + e * m
        for i in range(BLOCK):
            conf = 1.0 / den[i]
            depth = num[i] * conf
            put(depths, start + i, (conf * depth + row(pull_ref, i)) / (conf + row(coh_ref, i)))
        return 0

    lax.fori_loop(0, SEG // BLOCK, block, 0)

    for g in range(4):
        halves = [depths[pl.ds(half * 4 + g, SEG, stride=8), :] for half in range(2)]
        out[4 * g : 4 * g + 4] = jnp.concatenate(halves, axis=0).T.reshape(4, TILES, LANES)


def refine(own, mir):
    f32 = jnp.float32
    return pl.pallas_call(
        refine_kernel,
        out_shape=jax.ShapeDtypeStruct((CAMS, TILES, LANES), f32),
        in_specs=[pl.BlockSpec(memory_space=pltpu.VMEM)] * 2,
        out_specs=pl.BlockSpec(memory_space=pltpu.VMEM),
        scratch_shapes=[
            pltpu.VMEM((EXT * 8, LANES), f32),
            pltpu.VMEM((EXT * 8, LANES), f32),
            pltpu.VMEM((LANES * 8, LANES), f32),
            pltpu.VMEM((SEG * 8, LANES), f32),
            pltpu.VMEM((OFFS * BLOCK * 8, LANES), f32),
            pltpu.VMEM((BLOCK * 8, LANES), f32),
            pltpu.VMEM((BLOCK * 8, LANES), f32),
        ],
        compiler_params=pltpu.CompilerParams(vmem_limit_bytes=32 * 1024 * 1024),
        name="refine",
    )(own, mir)


def local(views, shifts):
    own, mir = exchange(views, shifts)
    return refine(own, mir).reshape(1, CAMS, 1, TILES * LANES)


def solution(mesh):
    placed = (P("vert", "au", None, None), P("vert", "au", None))
    return jax.shard_map(
        local, mesh=mesh, in_specs=placed, out_specs=P("vert", None, "au", None), check_vma=False
    )
```

```python
import functools
import math

import jax
import jax.numpy as jnp
from jax import lax
from jax.experimental import pallas as pl
from jax.experimental.pallas import tpu as pltpu
from jax.sharding import PartitionSpec as P

MAXS = 16
RAD = 2
OFFS = 2 * MAXS + 1
CAMS = 16
ROWS = 16
TILES = 32
LANES = 128
SEG = 64
HALO = MAXS + RAD
EXT = SEG + 2 * HALO
BLOCK = 8
SCALE = math.sqrt(0.5 * math.log2(math.e))
FAR = 1e30
MESH = pl.DeviceIdType.MESH


def spread(block, ref, first_row):
    for group in range(4):
        turned = block(group).T
        for half in range(2):
            ref[pl.ds(first_row * 8 + half * 4 + group, SEG, stride=8), :] = turned[half * SEG : (half + 1) * SEG]


def kernel(views, shifts, out, own, mir, band, flat, rows, shift_row, ext, facing, table, depths, costs, coh_ref, pull_ref,
           load_sem, zsend, zrecv, psend, precv, ready, ready_all, go):
    au = lax.axis_index("au")
    vert = lax.axis_index("vert")
    other = 30 - 2 * (vert // 2) + lax.rem(vert, 2)
    first = vert < 16

    load = pltpu.make_async_copy(views.at[0, 0], band, load_sem.at[0])
    load.start()
    load_shift = pltpu.make_async_copy(shifts.at[0], shift_row, load_sem.at[1])
    load_shift.start()

    def peer(k):
        return lax.rem(au + k, CAMS)

    def signal(sem, column, slot):
        pl.semaphore_signal(sem, inc=1, device_id={"au": column, "vert": slot}, device_id_type=MESH)

    def each(low, high, fn):
        def body(k, _):
            fn(k)
            return 0

        lax.fori_loop(low, high, body, 0)

    def across(k):
        return pltpu.make_async_remote_copy(
            src_ref=rows.at[peer(k), pl.ds(0, TILES)],
            dst_ref=mir.at[CAMS - 1 - au],
            send_sem=zsend.at[k],
            recv_sem=zrecv.at[k],
            device_id={"au": peer(k), "vert": other},
            device_id_type=MESH,
        )

    def inside(k):
        return pltpu.make_async_remote_copy(
            src_ref=rows.at[peer(k)],
            dst_ref=own.at[au],
            send_sem=psend.at[k],
            recv_sem=precv.at[k],
            device_id={"au": peer(k), "vert": vert},
            device_id_type=MESH,
        )

    barrier = pltpu.get_barrier_semaphore()

    @pl.when(first)
    def _():
        for k in range(1, CAMS):
            signal(barrier, peer(k), vert)

    load.wait()
    for t in range(TILES):
        flat[pl.ds(t, ROWS, stride=TILES), :] = band[:, t * LANES : (t + 1) * LANES].astype(jnp.float32)
    for y in range(ROWS):
        rows[y, 0:TILES, :] = flat[y * TILES : (y + 1) * TILES, :].astype(jnp.bfloat16)

    def fill():
        load_shift.wait()
        labels = jnp.concatenate([shift_row[...].astype(jnp.float32), jnp.zeros((1, LANES - 32), jnp.float32)], axis=1)
        labels = jnp.broadcast_to(labels, (16, LANES)).astype(jnp.bfloat16)
        for y in range(ROWS):
            rows[y, TILES : TILES + 16, :] = labels

    @pl.when(first)
    def _():
        pl.semaphore_wait(barrier, CAMS - 1)
        signal(barrier, au, other)
        fill()
        each(1, CAMS, lambda k: inside(k).start())
        pl.semaphore_wait(ready, 1)
        for k in range(1, CAMS):
            signal(ready_all, peer(k), vert)
        pl.semaphore_wait(ready_all, CAMS - 1)
        signal(go, au, other)
        each(0, CAMS, lambda k: across(k).start())

    @pl.when(jnp.logical_not(first))
    def _():
        pl.semaphore_wait(barrier, 1)
        each(0, CAMS, lambda k: across(k).start())
        signal(ready, au, other)
        fill()
        pl.semaphore_wait(go, 1)
        each(1, CAMS, lambda k: inside(k).start())

    keep = pltpu.make_async_copy(rows.at[au], own.at[au], load_sem.at[2])
    keep.start()
    keep.wait()
    each(1, CAMS, lambda k: inside(k).wait_recv())

    lane = lax.broadcasted_iota(jnp.int32, (8, LANES), 1)
    sub = lax.broadcasted_iota(jnp.int32, (8, LANES), 0)
    tile, member = lane % 32, lane // 32
    upper, group = sub >= 4, sub % 4
    zero = jnp.zeros((8, LANES), jnp.float32)

    def row(ref, i):
        if isinstance(i, int):
            return ref[i * 8 : i * 8 + 8, :]
        return ref[pl.ds(pl.multiple_of(i * 8, 8), 8), :]

    def put(ref, i, value):
        if isinstance(i, int):
            ref[i * 8 : i * 8 + 8, :] = value
        else:
            ref[pl.ds(pl.multiple_of(i * 8, 8), 8), :] = value

    def flat(ref, g):
        return ref[4 * g : 4 * g + 4, 0:TILES, :].astype(jnp.float32).reshape(LANES, LANES) * SCALE

    last_tile, first_tile = tile == TILES - 1, tile == 0
    def extend(source, ref):
        spread(functools.partial(flat, source), ref, HALO)
        for j in range(HALO):
            turned = pltpu.roll(row(ref, HALO + j), 4, 0)
            moved = jnp.where(last_tile, zero, pltpu.roll(turned, LANES - 1, 1))
            put(ref, HALO + SEG + j, jnp.where(upper, moved, turned))
            turned = pltpu.roll(row(ref, SEG + j), 4, 0)
            moved = jnp.where(first_tile, zero, pltpu.roll(turned, 1, 1))
            put(ref, j, jnp.where(upper, turned, moved))

    extend(own, ext)

    shift = own[:, TILES, :].astype(jnp.float32)
    offset = lax.broadcasted_iota(jnp.int32, (CAMS, LANES), 1).astype(jnp.float32) - MAXS
    often = jnp.zeros((CAMS, LANES), jnp.float32)
    total = jnp.zeros((CAMS, LANES), jnp.float32)
    for label in range(32):
        hit = shift[:, label : label + 1] == offset
        often = often + jnp.where(hit, 1.0, 0.0)
        total = total + jnp.where(hit, float(label), 0.0)
    both = often + pltpu.roll(total, 64, 1)

    def cams(g):
        return jnp.broadcast_to(both[4 * g : 4 * g + 4, None, :], (4, TILES, LANES)).reshape(LANES, LANES)

    for g in range(4):
        turned = cams(g).T
        for half in range(2):
            table[pl.ds(half * 4 + g, LANES, stride=8), :] = turned

    def after(value):
        a = pltpu.roll(value, LANES - 32, 1)
        b = jnp.where(group < 3, pltpu.roll(a, 7, 0), zero)
        return jnp.where(member < 3, a, b)

    def before(value):
        a = pltpu.roll(value, 32, 1)
        b = jnp.where(group > 0, pltpu.roll(a, 1, 0), zero)
        return jnp.where(member > 0, a, b)

    def boxed(values):
        pairs = [values[i] + values[i + 1] for i in range(len(values) - 1)]
        return [pairs[i] + pairs[i + 2] + values[i + 4] for i in range(len(values) - 4)]

    outside_left = jnp.logical_and(first_tile, jnp.logical_not(upper))
    outside_right = jnp.logical_and(last_tile, upper)

    def epipolar(b, _):
        start = b * BLOCK
        left = jnp.where(jnp.logical_and(outside_left, b == 0), zero, zero + 1.0)
        right = jnp.where(jnp.logical_and(outside_right, b == SEG // BLOCK - 1), zero, zero + 1.0)

        def inside(values):
            return [v * left for v in values[:RAD]] + values[RAD:-RAD] + [v * right for v in values[-RAD:]]

        base = start + HALO - RAD
        width = BLOCK + 2 * RAD
        gx = inside([row(ext, base + i + 1) - row(ext, base + i - 1) for i in range(width)])
        gu = [after(row(ext, base + i)) - before(row(ext, base + i)) for i in range(width)]
        xx = boxed([g * g for g in gx])
        xu = boxed([g * h for g, h in zip(gx, gu)])
        unit = 0.25 / (SCALE * SCALE)
        cohs, pulls = [], []
        for i in range(BLOCK):
            jxx = (xx[i] + after(xx[i]) + before(xx[i])) * unit
            jxu = (xu[i] + after(xu[i]) + before(xu[i])) * unit
            inv = 1.0 / (jxx + 1.0)
            coh = jxx * inv
            put(coh_ref, start + i, coh)
            put(pull_ref, start + i, 4.0 * coh * (-jxu * inv))

        return 0

    lax.fori_loop(0, SEG // BLOCK, epipolar, 0)
    each(0, CAMS, lambda k: across(k).wait_recv())
    extend(mir, facing)

    def block(b, _):
        start = b * BLOCK
        left = jnp.where(jnp.logical_and(outside_left, b == 0), zero, zero + 1.0)
        right = jnp.where(jnp.logical_and(outside_right, b == SEG // BLOCK - 1), zero, zero + 1.0)

        def inside(values):
            return [v * left for v in values[:RAD]] + values[RAD:-RAD] + [v * right for v in values[-RAD:]]

        base = start + HALO - RAD
        width = BLOCK + 2 * RAD
        best = [zero + FAR for _ in range(BLOCK)]
        for s in range(OFFS):
            step = s - MAXS
            squares = []
            for i in range(width):
                d = row(ext, base + i + step) - row(facing, base + i - step)
                squares.append(d * d)
            miss = jnp.where(row(table, s) > 0.0, 0.0, FAR)
            for i, cost in enumerate(boxed(inside(squares))):
                cost = cost + miss
                put(costs, s * BLOCK + i, cost)
                best[i] = jnp.minimum(best[i], cost)
        den = [zero for _ in range(BLOCK)]
        num = [zero for _ in range(BLOCK)]
        for s in range(OFFS):
            n, m = row(table, s), row(table, 64 + s)
            for i in range(BLOCK):
                e = jnp.exp2(best[i] - row(costs, s * BLOCK + i))
                den[i] = den[i] + e * n
                num[i] = num[i] + e * m
        for i in range(BLOCK):
            conf = 1.0 / den[i]
            depth = num[i] * conf
            put(depths, start + i, (conf * depth + row(pull_ref, start + i)) / (conf + row(coh_ref, start + i)))
        return 0

    lax.fori_loop(0, SEG // BLOCK, block, 0)

    for g in range(4):
        halves = [depths[pl.ds(half * 4 + g, SEG, stride=8), :] for half in range(2)]
        out[4 * g : 4 * g + 4] = jnp.concatenate(halves, axis=0).T.reshape(4, TILES, LANES)

    each(0, CAMS, lambda k: across(k).wait_send())
    each(1, CAMS, lambda k: inside(k).wait_send())


def local(views, shifts):
    f32, bf16 = jnp.float32, jnp.bfloat16
    dma = pltpu.SemaphoreType.DMA
    out = pl.pallas_call(
        kernel,
        out_shape=jax.ShapeDtypeStruct((CAMS, TILES, LANES), f32),
        in_specs=[pl.BlockSpec(memory_space=pltpu.HBM)] * 2,
        out_specs=pl.BlockSpec(memory_space=pltpu.VMEM),
        scratch_shapes=[
            pltpu.VMEM((CAMS, TILES + 16, LANES), bf16),
            pltpu.VMEM((CAMS, TILES, LANES), bf16),
            pltpu.VMEM((ROWS, TILES * LANES), bf16),
            pltpu.VMEM((ROWS * TILES, LANES), f32),
            pltpu.VMEM((ROWS, TILES + 16, LANES), bf16),
            pltpu.VMEM((1, 32), jnp.int32),
            pltpu.VMEM((EXT * 8, LANES), f32),
            pltpu.VMEM((EXT * 8, LANES), f32),
            pltpu.VMEM((LANES * 8, LANES), f32),
            pltpu.VMEM((SEG * 8, LANES), f32),
            pltpu.VMEM((OFFS * BLOCK * 8, LANES), f32),
            pltpu.VMEM((SEG * 8, LANES), f32),
            pltpu.VMEM((SEG * 8, LANES), f32),
            dma((3,)),
            dma((CAMS,)),
            dma((CAMS,)),
            dma((CAMS,)),
            dma((CAMS,)),
            pltpu.SemaphoreType.REGULAR,
            pltpu.SemaphoreType.REGULAR,
            pltpu.SemaphoreType.REGULAR,
        ],
        compiler_params=pltpu.CompilerParams(
            collective_id=0, has_side_effects=True, vmem_limit_bytes=32 * 1024 * 1024
        ),
        name="light_field",
    )(*[pltpu.with_memory_space_constraint(a, pltpu.HBM) for a in (views, shifts)])
    return out.reshape(1, CAMS, 1, TILES * LANES)


def solution(mesh):
    placed = (P("vert", "au", None, None), P("vert", "au", None))
    return jax.shard_map(
        local, mesh=mesh, in_specs=placed, out_specs=P("vert", None, "au", None), check_vma=False
    )
```

```python
import functools
import math

import jax
import jax.numpy as jnp
from jax import lax
from jax.experimental import pallas as pl
from jax.experimental.pallas import tpu as pltpu
from jax.sharding import PartitionSpec as P

MAXS = 16
RAD = 2
OFFS = 2 * MAXS + 1
CAMS = 16
ROWS = 16
TILES = 32
LANES = 128
SEG = 16
HALO = MAXS + RAD
EXT = SEG + 2 * HALO
SCALE = math.sqrt(0.5 * math.log2(math.e))
FAR = 1e30
MESH = pl.DeviceIdType.MESH


def kernel(views, shifts, out, own, mir, band, flat, rows, shift_row, bare, xx_ref, xu_ref, coh_ref, pull_ref, both_ref,
           turned, ext, facing, table, coh_chunk, pull_chunk, costs, result,
           load_sem, zsend, zrecv, psend, precv, ready, ready_all, go):
    au = lax.axis_index("au")
    vert = lax.axis_index("vert")
    other = 30 - 2 * (vert // 2) + lax.rem(vert, 2)
    first = vert < 16
    middle = jnp.logical_and(vert >= 6, vert < 26)
    flight = CAMS
    for slot, count in ((24, 2), (26, 8), (28, 8), (30, 6)):
        flight = jnp.where(jnp.logical_and(vert >= slot, vert < slot + 2), count, flight)

    load = pltpu.make_async_copy(views.at[0, 0], band, load_sem.at[0])
    load.start()
    load_shift = pltpu.make_async_copy(shifts.at[0], shift_row, load_sem.at[1])
    load_shift.start()

    def peer(k):
        return lax.rem(au + k, CAMS)

    def signal(sem, column, slot):
        pl.semaphore_signal(sem, inc=1, device_id={"au": column, "vert": slot}, device_id_type=MESH)

    def each(low, high, fn, unroll=None):
        def body(k, _):
            fn(k)
            return 0

        lax.fori_loop(low, high, body, 0, unroll=unroll)

    def across(k):
        return pltpu.make_async_remote_copy(
            src_ref=rows.at[peer(k), pl.ds(0, TILES)],
            dst_ref=mir.at[k],
            send_sem=zsend.at[k],
            recv_sem=zrecv.at[k],
            device_id={"au": peer(k), "vert": other},
            device_id_type=MESH,
        )

    def inside(k):
        return pltpu.make_async_remote_copy(
            src_ref=rows.at[peer(k)],
            dst_ref=own.at[au],
            send_sem=psend.at[k],
            recv_sem=precv.at[k],
            device_id={"au": peer(k), "vert": vert},
            device_id_type=MESH,
        )

    def rest(k):
        across(k - flight).wait_send()
        across(k).start()

    barrier = pltpu.get_barrier_semaphore()

    @pl.when(jnp.logical_or(first, middle))
    def _():
        for k in range(1, CAMS):
            signal(barrier, peer(k), vert)

    load.wait()
    for t in range(TILES):
        flat[pl.ds(t, ROWS, stride=TILES), :] = band[:, t * LANES : (t + 1) * LANES].astype(jnp.float32)
    for y in range(ROWS):
        rows[y, 0:TILES, :] = flat[y * TILES : (y + 1) * TILES, :].astype(jnp.bfloat16)

    def fill():
        load_shift.wait()
        labels = jnp.concatenate([shift_row[...].astype(jnp.float32), jnp.zeros((1, LANES - 32), jnp.float32)], axis=1)
        labels = jnp.broadcast_to(labels, (16, LANES)).astype(jnp.bfloat16)
        for y in range(ROWS):
            rows[y, TILES : TILES + 16, :] = labels

    @pl.when(first)
    def _():
        pl.semaphore_wait(barrier, CAMS - 1)
        signal(barrier, au, other)
        fill()
        each(1, CAMS, lambda k: inside(k).start())
        pl.semaphore_wait(ready, 1)

        @pl.when(jnp.logical_not(middle))
        def _():
            for k in range(1, CAMS):
                signal(ready_all, peer(k), vert)
            pl.semaphore_wait(ready_all, CAMS - 1)
            signal(go, au, other)

        each(0, flight, lambda k: across(k).start())

    @pl.when(jnp.logical_not(first))
    def _():
        @pl.when(middle)
        def _():
            pl.semaphore_wait(barrier, CAMS)

        @pl.when(jnp.logical_not(middle))
        def _():
            pl.semaphore_wait(barrier, 1)

        each(0, flight, lambda k: across(k).start())
        signal(ready, au, other)
        fill()

        @pl.when(jnp.logical_not(middle))
        def _():
            pl.semaphore_wait(go, 1)

        each(1, CAMS, lambda k: inside(k).start())

        each(flight, CAMS, rest)

    keep = pltpu.make_async_copy(rows.at[au], own.at[au], load_sem.at[2])
    keep.start()
    keep.wait()
    each(1, CAMS, lambda k: inside(k).wait_recv())

    blank = jnp.zeros((TILES, LANES), jnp.float32)
    wide_lane = lax.broadcasted_iota(jnp.int32, (TILES, LANES), 1)
    wide_tile = lax.broadcasted_iota(jnp.int32, (TILES, LANES), 0)

    def ahead(value, d):
        a = pltpu.roll(value, LANES - d, 1)
        b = jnp.where(wide_tile == TILES - 1, blank, pltpu.roll(a, TILES - 1, 0))
        return jnp.where(wide_lane >= LANES - d, b, a)

    def behind(value, d):
        a = pltpu.roll(value, d, 1)
        b = jnp.where(wide_tile == 0, blank, pltpu.roll(a, 1, 0))
        return jnp.where(wide_lane < d, b, a)

    def at(a):
        return pl.ds(pl.multiple_of((a + 1) * TILES, TILES), TILES)

    for ref in (bare, xx_ref, xu_ref):
        ref[0:TILES, :] = blank
        ref[(CAMS + 1) * TILES : (CAMS + 2) * TILES, :] = blank
    bare[TILES : (CAMS + 1) * TILES, :] = own[:, 0:TILES, :].astype(jnp.float32).reshape(CAMS * TILES, LANES)

    def gradients(a):
        value = bare[at(a), :]
        gx = ahead(value, 1) - behind(value, 1)
        gu = bare[at(a + 1), :] - bare[at(a - 1), :]
        xx_ref[at(a), :] = gx * gx
        xu_ref[at(a), :] = gx * gu

    each(0, CAMS, gradients, 4)

    def boxes(a):
        def box(ref):
            value = ref[at(a - 1), :] + ref[at(a), :] + ref[at(a + 1), :]
            return (behind(value, 2) + behind(value, 1) + value + ahead(value, 1) + ahead(value, 2)) * 0.25

        jxx, jxu = box(xx_ref), box(xu_ref)
        inv = 1.0 / (jxx + 1.0)
        coh = jxx * inv
        coh_ref[at(a - 1), :] = coh
        pull_ref[at(a - 1), :] = 4.0 * coh * (-jxu * inv)

    each(0, CAMS, boxes, 4)

    shift = own[:, TILES, :].astype(jnp.float32)
    offset = lax.broadcasted_iota(jnp.int32, (CAMS, LANES), 1).astype(jnp.float32) - MAXS
    often = jnp.zeros((CAMS, LANES), jnp.float32)
    total = jnp.zeros((CAMS, LANES), jnp.float32)
    for label in range(32):
        hit = shift[:, label : label + 1] == offset
        often = often + jnp.where(hit, 1.0, 0.0)
        total = total + jnp.where(hit, float(label), 0.0)
    both_ref[...] = often + pltpu.roll(total, 64, 1)

    lane = lax.broadcasted_iota(jnp.int32, (8, LANES), 1)
    sub = lax.broadcasted_iota(jnp.int32, (8, LANES), 0)
    first_tile, last_tile = lane % 32 == 0, lane % 32 == TILES - 1
    zero = jnp.zeros((8, LANES), jnp.float32)

    def right_of(value):
        a = pltpu.roll(value, 7, 0)
        b = jnp.where(last_tile, zero, pltpu.roll(a, LANES - 1, 1))
        return jnp.where(sub == 7, b, a)

    def left_of(value):
        a = pltpu.roll(value, 1, 0)
        b = jnp.where(first_tile, zero, pltpu.roll(a, 1, 1))
        return jnp.where(sub == 0, b, a)

    def camera(g, j):
        return lax.rem(2 * CAMS - 1 - au + 4 * g + j, CAMS)

    def put(ref, start, i, value):
        ref[pl.ds(pl.multiple_of((start + i) * 8, 8), 8), :] = value

    def get(ref, start, i):
        return ref[pl.ds(pl.multiple_of((start + i) * 8, 8), 8), :]

    def extend(block, ref, start):
        turned[...] = (block * SCALE).T
        values = [turned[pl.ds(i, 8, stride=SEG), :] for i in range(SEG)]
        right = [right_of(v) for v in values]
        right += [right_of(v) for v in right[:RAD]]
        left = [left_of(v) for v in values]
        left = [left_of(v) for v in left[-RAD:]] + left
        for i, value in enumerate(left + values + right):
            put(ref, start, i, value)

    def prepare(g):
        cams = [camera(g, j) for j in range(4)]

        def natural(ref):
            return jnp.concatenate([ref[pl.ds(pl.multiple_of(c * TILES, TILES), TILES), :] for c in cams], axis=0)

        block = jnp.concatenate([bare[at(c), :] for c in cams], axis=0)
        extend(block, ext, g * EXT)
        here = pl.ds(pl.multiple_of(g * LANES, LANES), LANES)
        coh_chunk[here, :] = natural(coh_ref).T
        pull_chunk[here, :] = natural(pull_ref).T
        labels = [jnp.broadcast_to(both_ref[pl.ds(c, 1), :], (TILES, LANES)) for c in cams]
        table[here, :] = jnp.concatenate(labels, axis=0).T

    each(0, 4, prepare)

    @pl.when(first)
    def _():
        each(flight, CAMS, rest)

    outside_left = jnp.where(jnp.logical_and(first_tile, sub == 0), 0.0, 1.0)
    outside_right = jnp.where(jnp.logical_and(last_tile, sub == 7), 0.0, 1.0)

    def boxed(values):
        pairs = [values[i] + values[i + 1] for i in range(len(values) - 1)]
        return [pairs[i] + pairs[i + 2] + values[i + 4] for i in range(len(values) - 4)]

    def chunk(g):
        each(0, 4, lambda j: across(4 * g + j).wait_recv())

        extend(mir[pl.ds(4 * g, 4), :, :].astype(jnp.float32).reshape(LANES, LANES), facing, 0)

        def entry(s):
            return jnp.broadcast_to(table[pl.ds(g * LANES + s, 1), :], (8, LANES))

        best = [zero + FAR for _ in range(SEG)]
        for s in range(OFFS):
            step = s - MAXS
            squares = []
            for i in range(SEG + 2 * RAD):
                d = get(ext, g * EXT, HALO - RAD + i + step) - get(facing, 0, HALO - RAD + i - step)
                squares.append(d * d)
            squares[:RAD] = [q * outside_left for q in squares[:RAD]]
            squares[-RAD:] = [q * outside_right for q in squares[-RAD:]]
            miss = jnp.where(entry(s) > 0.0, 0.0, FAR)
            for i, cost in enumerate(boxed(squares)):
                cost = cost + miss
                put(costs, s * SEG, i, cost)
                best[i] = jnp.minimum(best[i], cost)
        den = [zero for _ in range(SEG)]
        num = [zero for _ in range(SEG)]
        for s in range(OFFS):
            n, m = entry(s), entry(64 + s)
            for i in range(SEG):
                e = jnp.exp2(best[i] - get(costs, s * SEG, i))
                den[i] = den[i] + e * n
                num[i] = num[i] + e * m
        for i in range(SEG):
            here = pl.ds(g * LANES + i, 8, stride=SEG)
            conf = 1.0 / den[i]
            depth = num[i] * conf
            value = (conf * depth + pull_chunk[here, :]) / (conf + coh_chunk[here, :])
            result[pl.ds(i, 8, stride=SEG), :] = value
        back = result[...].T
        for j in range(4):
            out[camera(g, j)] = back[j * TILES : (j + 1) * TILES]

    each(0, 4, chunk)

    each(CAMS - flight, CAMS, lambda k: across(k).wait_send())
    each(1, CAMS, lambda k: inside(k).wait_send())


def local(views, shifts):
    f32, bf16 = jnp.float32, jnp.bfloat16
    dma = pltpu.SemaphoreType.DMA
    out = pl.pallas_call(
        kernel,
        out_shape=jax.ShapeDtypeStruct((CAMS, TILES, LANES), f32),
        in_specs=[pl.BlockSpec(memory_space=pltpu.HBM)] * 2,
        out_specs=pl.BlockSpec(memory_space=pltpu.VMEM),
        scratch_shapes=[
            pltpu.VMEM((CAMS, TILES + 16, LANES), bf16),
            pltpu.VMEM((CAMS, TILES, LANES), bf16),
            pltpu.VMEM((ROWS, TILES * LANES), bf16),
            pltpu.VMEM((ROWS * TILES, LANES), f32),
            pltpu.VMEM((ROWS, TILES + 16, LANES), bf16),
            pltpu.VMEM((1, 32), jnp.int32),
            pltpu.VMEM(((CAMS + 2) * TILES, LANES), f32),
            pltpu.VMEM(((CAMS + 2) * TILES, LANES), f32),
            pltpu.VMEM(((CAMS + 2) * TILES, LANES), f32),
            pltpu.VMEM((CAMS * TILES, LANES), f32),
            pltpu.VMEM((CAMS * TILES, LANES), f32),
            pltpu.VMEM((CAMS, LANES), f32),
            pltpu.VMEM((LANES, LANES), f32),
            pltpu.VMEM((4 * EXT * 8, LANES), f32),
            pltpu.VMEM((EXT * 8, LANES), f32),
            pltpu.VMEM((4 * LANES, LANES), f32),
            pltpu.VMEM((4 * LANES, LANES), f32),
            pltpu.VMEM((4 * LANES, LANES), f32),
            pltpu.VMEM((OFFS * SEG * 8, LANES), f32),
            pltpu.VMEM((LANES, LANES), f32),
            dma((3,)),
            dma((CAMS,)),
            dma((CAMS,)),
            dma((CAMS,)),
            dma((CAMS,)),
            pltpu.SemaphoreType.REGULAR,
            pltpu.SemaphoreType.REGULAR,
            pltpu.SemaphoreType.REGULAR,
        ],
        compiler_params=pltpu.CompilerParams(
            collective_id=0, has_side_effects=True, vmem_limit_bytes=32 * 1024 * 1024
        ),
        name="light_field",
    )(*[pltpu.with_memory_space_constraint(a, pltpu.HBM) for a in (views, shifts)])
    return out.reshape(1, CAMS, 1, TILES * LANES)


def solution(mesh):
    placed = (P("vert", "au", None, None), P("vert", "au", None))
    return jax.shard_map(
        local, mesh=mesh, in_specs=placed, out_specs=P("vert", None, "au", None), check_vma=False
    )
```

```python
import functools
import math

import jax
import jax.numpy as jnp
from jax import lax
from jax.experimental import pallas as pl
from jax.experimental.pallas import tpu as pltpu
from jax.sharding import PartitionSpec as P

MAXS = 16
RAD = 2
OFFS = 2 * MAXS + 1
CAMS = 16
ROWS = 16
TILES = 32
LANES = 128
SEG = 16
HALO = MAXS + RAD
EXT = SEG + 2 * HALO
SCALE = math.sqrt(0.5 * math.log2(math.e))
FAR = 1e30
MESH = pl.DeviceIdType.MESH


def kernel(views, shifts, out, own, mir, band, flat, rows, shift_row, bare, xx_ref, xu_ref, coh_ref, pull_ref, both_ref,
           turned, ext, facing, table, coh_chunk, pull_chunk, costs, result,
           load_sem, zsend, zrecv, psend, precv, ready, ready_all, go):
    au = lax.axis_index("au")
    vert = lax.axis_index("vert")
    other = 30 - 2 * (vert // 2) + lax.rem(vert, 2)
    first = vert < 16
    middle = jnp.logical_and(vert >= 6, vert < 26)
    flight = CAMS
    for slot, count in ((24, 3), (26, 10), (28, 8), (30, 6), (6, 8)):
        flight = jnp.where(jnp.logical_and(vert >= slot, vert < slot + 2), count, flight)

    load = pltpu.make_async_copy(views.at[0, 0], band, load_sem.at[0])
    load.start()
    load_shift = pltpu.make_async_copy(shifts.at[0], shift_row, load_sem.at[1])
    load_shift.start()

    def peer(k):
        return lax.rem(au + k, CAMS)

    def signal(sem, column, slot):
        pl.semaphore_signal(sem, inc=1, device_id={"au": column, "vert": slot}, device_id_type=MESH)

    def each(low, high, fn, unroll=None):
        def body(k, _):
            fn(k)
            return 0

        lax.fori_loop(low, high, body, 0, unroll=unroll)

    ahead_of = lax.rem(CAMS + 1 - au, CAMS)

    def across(i):
        k = jnp.where(i == 0, ahead_of, jnp.where(i <= ahead_of, i - 1, i))
        return pltpu.make_async_remote_copy(
            src_ref=rows.at[peer(k), pl.ds(0, TILES)],
            dst_ref=mir.at[k],
            send_sem=zsend.at[k],
            recv_sem=zrecv.at[k],
            device_id={"au": peer(k), "vert": other},
            device_id_type=MESH,
        )

    def arrival(k):
        return pltpu.make_async_remote_copy(
            src_ref=rows.at[au, pl.ds(0, TILES)],
            dst_ref=mir.at[k],
            send_sem=zsend.at[k],
            recv_sem=zrecv.at[k],
            device_id={"au": au, "vert": other},
            device_id_type=MESH,
        )

    def inside(k):
        return pltpu.make_async_remote_copy(
            src_ref=rows.at[peer(k)],
            dst_ref=own.at[au],
            send_sem=psend.at[k],
            recv_sem=precv.at[k],
            device_id={"au": peer(k), "vert": vert},
            device_id_type=MESH,
        )

    def rest(k):
        across(k - flight).wait_send()
        across(k).start()

    barrier = pltpu.get_barrier_semaphore()

    @pl.when(jnp.logical_or(first, middle))
    def _():
        for k in range(1, CAMS):
            signal(barrier, peer(k), vert)

    load.wait()
    for t in range(TILES):
        flat[pl.ds(t, ROWS, stride=TILES), :] = band[:, t * LANES : (t + 1) * LANES].astype(jnp.float32)
    for y in range(ROWS):
        rows[y, 0:TILES, :] = flat[y * TILES : (y + 1) * TILES, :].astype(jnp.bfloat16)

    def fill():
        load_shift.wait()
        labels = jnp.concatenate([shift_row[...].astype(jnp.float32), jnp.zeros((1, LANES - 32), jnp.float32)], axis=1)
        labels = jnp.broadcast_to(labels, (16, LANES)).astype(jnp.bfloat16)
        for y in range(ROWS):
            rows[y, TILES : TILES + 16, :] = labels

    @pl.when(first)
    def _():
        pl.semaphore_wait(barrier, CAMS - 1)
        signal(barrier, au, other)
        fill()
        each(1, CAMS, lambda k: inside(k).start())
        pl.semaphore_wait(ready, 1)

        @pl.when(jnp.logical_not(middle))
        def _():
            for k in range(1, CAMS):
                signal(ready_all, peer(k), vert)
            pl.semaphore_wait(ready_all, CAMS - 1)
            signal(go, au, other)

        each(0, flight, lambda k: across(k).start())

    @pl.when(jnp.logical_not(first))
    def _():
        @pl.when(middle)
        def _():
            pl.semaphore_wait(barrier, CAMS)

        @pl.when(jnp.logical_not(middle))
        def _():
            pl.semaphore_wait(barrier, 1)

        signal(ready, au, other)
        each(0, flight, lambda k: across(k).start())
        fill()

        @pl.when(jnp.logical_not(middle))
        def _():
            pl.semaphore_wait(go, 1)

        each(1, CAMS, lambda k: inside(k).start())

        each(flight, CAMS, rest)

    keep = pltpu.make_async_copy(rows.at[au], own.at[au], load_sem.at[2])
    keep.start()
    keep.wait()
    each(1, CAMS, lambda k: inside(k).wait_recv())

    blank = jnp.zeros((TILES, LANES), jnp.float32)
    wide_lane = lax.broadcasted_iota(jnp.int32, (TILES, LANES), 1)
    wide_tile = lax.broadcasted_iota(jnp.int32, (TILES, LANES), 0)

    def ahead(value, d):
        a = pltpu.roll(value, LANES - d, 1)
        b = jnp.where(wide_tile == TILES - 1, blank, pltpu.roll(a, TILES - 1, 0))
        return jnp.where(wide_lane >= LANES - d, b, a)

    def behind(value, d):
        a = pltpu.roll(value, d, 1)
        b = jnp.where(wide_tile == 0, blank, pltpu.roll(a, 1, 0))
        return jnp.where(wide_lane < d, b, a)

    def at(a):
        return pl.ds(pl.multiple_of((a + 1) * TILES, TILES), TILES)

    for ref in (bare, xx_ref, xu_ref):
        ref[0:TILES, :] = blank
        ref[(CAMS + 1) * TILES : (CAMS + 2) * TILES, :] = blank
    bare[TILES : (CAMS + 1) * TILES, :] = own[:, 0:TILES, :].astype(jnp.float32).reshape(CAMS * TILES, LANES)

    def gradients(a):
        value = bare[at(a), :]
        gx = ahead(value, 1) - behind(value, 1)
        gu = bare[at(a + 1), :] - bare[at(a - 1), :]
        xx_ref[at(a), :] = gx * gx
        xu_ref[at(a), :] = gx * gu

    each(0, CAMS, gradients, 4)

    def boxes(a):
        def box(ref):
            value = ref[at(a - 1), :] + ref[at(a), :] + ref[at(a + 1), :]
            return (behind(value, 2) + behind(value, 1) + value + ahead(value, 1) + ahead(value, 2)) * 0.25

        jxx, jxu = box(xx_ref), box(xu_ref)
        inv = 1.0 / (jxx + 1.0)
        coh = jxx * inv
        coh_ref[at(a - 1), :] = coh
        pull_ref[at(a - 1), :] = 4.0 * coh * (-jxu * inv)

    each(0, CAMS, boxes, 4)

    shift = own[:, TILES, :].astype(jnp.float32)
    offset = lax.broadcasted_iota(jnp.int32, (CAMS, LANES), 1).astype(jnp.float32) - MAXS
    often = jnp.zeros((CAMS, LANES), jnp.float32)
    total = jnp.zeros((CAMS, LANES), jnp.float32)
    for label in range(32):
        hit = shift[:, label : label + 1] == offset
        often = often + jnp.where(hit, 1.0, 0.0)
        total = total + jnp.where(hit, float(label), 0.0)
    both_ref[...] = often + pltpu.roll(total, 64, 1)

    lane = lax.broadcasted_iota(jnp.int32, (8, LANES), 1)
    sub = lax.broadcasted_iota(jnp.int32, (8, LANES), 0)
    first_tile, last_tile = lane % 32 == 0, lane % 32 == TILES - 1
    zero = jnp.zeros((8, LANES), jnp.float32)

    def right_of(value):
        a = pltpu.roll(value, 7, 0)
        b = jnp.where(last_tile, zero, pltpu.roll(a, LANES - 1, 1))
        return jnp.where(sub == 7, b, a)

    def left_of(value):
        a = pltpu.roll(value, 1, 0)
        b = jnp.where(first_tile, zero, pltpu.roll(a, 1, 1))
        return jnp.where(sub == 0, b, a)

    def camera(g, j):
        return lax.rem(2 * CAMS - 1 - au + 4 * g + j, CAMS)

    def put(ref, start, i, value):
        ref[pl.ds(pl.multiple_of((start + i) * 8, 8), 8), :] = value

    def get(ref, start, i):
        return ref[pl.ds(pl.multiple_of((start + i) * 8, 8), 8), :]

    def extend(block, ref, start):
        turned[...] = (block * SCALE).T
        values = [turned[pl.ds(i, 8, stride=SEG), :] for i in range(SEG)]
        right = [right_of(v) for v in values]
        right += [right_of(v) for v in right[:RAD]]
        left = [left_of(v) for v in values]
        left = [left_of(v) for v in left[-RAD:]] + left
        for i, value in enumerate(left + values + right):
            put(ref, start, i, value)

    def prepare(g):
        cams = [camera(g, j) for j in range(4)]

        def natural(ref):
            return jnp.concatenate([ref[pl.ds(pl.multiple_of(c * TILES, TILES), TILES), :] for c in cams], axis=0)

        block = jnp.concatenate([bare[at(c), :] for c in cams], axis=0)
        extend(block, ext, g * EXT)
        here = pl.ds(pl.multiple_of(g * LANES, LANES), LANES)
        coh_chunk[here, :] = natural(coh_ref).T
        pull_chunk[here, :] = natural(pull_ref).T
        labels = [jnp.broadcast_to(both_ref[pl.ds(c, 1), :], (TILES, LANES)) for c in cams]
        table[here, :] = jnp.concatenate(labels, axis=0).T

    each(0, 4, prepare)

    @pl.when(first)
    def _():
        each(flight, CAMS, rest)

    outside_left = jnp.where(jnp.logical_and(first_tile, sub == 0), 0.0, 1.0)
    outside_right = jnp.where(jnp.logical_and(last_tile, sub == 7), 0.0, 1.0)

    def boxed(values):
        sums = []
        for i in range(len(values) - 4):
            if i % 8 == 0:
                sums.append((values[i] + values[i + 1]) + (values[i + 2] + values[i + 3]) + values[i + 4])
            else:
                sums.append(sums[-1] + (values[i + 4] - values[i - 1]))
        return sums

    def chunk(g):
        each(0, 4, lambda j: arrival(4 * g + j).wait_recv())

        extend(mir[pl.ds(4 * g, 4), :, :].astype(jnp.float32).reshape(LANES, LANES), facing, 0)

        def entry(s):
            return jnp.broadcast_to(table[pl.ds(g * LANES + s, 1), :], (8, LANES))

        best = [zero + FAR for _ in range(SEG)]
        for s in range(OFFS):
            step = s - MAXS
            squares = []
            for i in range(SEG + 2 * RAD):
                d = get(ext, g * EXT, HALO - RAD + i + step) - get(facing, 0, HALO - RAD + i - step)
                squares.append(d * d)
            squares[:RAD] = [q * outside_left for q in squares[:RAD]]
            squares[-RAD:] = [q * outside_right for q in squares[-RAD:]]
            miss = jnp.where(entry(s) > 0.0, 0.0, FAR)
            for i, cost in enumerate(boxed(squares)):
                cost = cost + miss
                put(costs, s * SEG, i, cost)
                best[i] = jnp.minimum(best[i], cost)
        den = [zero for _ in range(SEG)]
        num = [zero for _ in range(SEG)]
        for s in range(OFFS):
            n, m = entry(s), entry(64 + s)
            for i in range(SEG):
                e = jnp.exp2(best[i] - get(costs, s * SEG, i))
                den[i] = den[i] + e * n
                num[i] = num[i] + e * m
        for i in range(SEG):
            here = pl.ds(g * LANES + i, 8, stride=SEG)
            conf = 1.0 / den[i]
            depth = num[i] * conf
            value = (conf * depth + pull_chunk[here, :]) / (conf + coh_chunk[here, :])
            result[pl.ds(i, 8, stride=SEG), :] = value
        back = result[...].T
        for j in range(4):
            out[camera(g, j)] = back[j * TILES : (j + 1) * TILES]

    each(0, 4, chunk)

    each(CAMS - flight, CAMS, lambda k: across(k).wait_send())
    each(1, CAMS, lambda k: inside(k).wait_send())


def local(views, shifts):
    f32, bf16 = jnp.float32, jnp.bfloat16
    dma = pltpu.SemaphoreType.DMA
    out = pl.pallas_call(
        kernel,
        out_shape=jax.ShapeDtypeStruct((CAMS, TILES, LANES), f32),
        in_specs=[pl.BlockSpec(memory_space=pltpu.HBM)] * 2,
        out_specs=pl.BlockSpec(memory_space=pltpu.VMEM),
        scratch_shapes=[
            pltpu.VMEM((CAMS, TILES + 16, LANES), bf16),
            pltpu.VMEM((CAMS, TILES, LANES), bf16),
            pltpu.VMEM((ROWS, TILES * LANES), bf16),
            pltpu.VMEM((ROWS * TILES, LANES), f32),
            pltpu.VMEM((ROWS, TILES + 16, LANES), bf16),
            pltpu.VMEM((1, 32), jnp.int32),
            pltpu.VMEM(((CAMS + 2) * TILES, LANES), f32),
            pltpu.VMEM(((CAMS + 2) * TILES, LANES), f32),
            pltpu.VMEM(((CAMS + 2) * TILES, LANES), f32),
            pltpu.VMEM((CAMS * TILES, LANES), f32),
            pltpu.VMEM((CAMS * TILES, LANES), f32),
            pltpu.VMEM((CAMS, LANES), f32),
            pltpu.VMEM((LANES, LANES), f32),
            pltpu.VMEM((4 * EXT * 8, LANES), f32),
            pltpu.VMEM((EXT * 8, LANES), f32),
            pltpu.VMEM((4 * LANES, LANES), f32),
            pltpu.VMEM((4 * LANES, LANES), f32),
            pltpu.VMEM((4 * LANES, LANES), f32),
            pltpu.VMEM((OFFS * SEG * 8, LANES), f32),
            pltpu.VMEM((LANES, LANES), f32),
            dma((3,)),
            dma((CAMS,)),
            dma((CAMS,)),
            dma((CAMS,)),
            dma((CAMS,)),
            pltpu.SemaphoreType.REGULAR,
            pltpu.SemaphoreType.REGULAR,
            pltpu.SemaphoreType.REGULAR,
        ],
        compiler_params=pltpu.CompilerParams(
            collective_id=0, has_side_effects=True, vmem_limit_bytes=32 * 1024 * 1024
        ),
        name="light_field",
    )(*[pltpu.with_memory_space_constraint(a, pltpu.HBM) for a in (views, shifts)])
    return out.reshape(1, CAMS, 1, TILES * LANES)


def solution(mesh):
    placed = (P("vert", "au", None, None), P("vert", "au", None))
    return jax.shard_map(
        local, mesh=mesh, in_specs=placed, out_specs=P("vert", None, "au", None), check_vma=False
    )
```

```python
import functools
import math

import jax
import jax.numpy as jnp
from jax import lax
from jax.experimental import pallas as pl
from jax.experimental.pallas import tpu as pltpu
from jax.sharding import PartitionSpec as P

MAXS = 16
RAD = 2
OFFS = 2 * MAXS + 1
CAMS = 16
ROWS = 16
TILES = 32
LANES = 128
SEG = 16
HALO = MAXS + RAD
EXT = SEG + 2 * HALO
SCALE = math.sqrt(0.5 * math.log2(math.e))
FAR = 1e30
MESH = pl.DeviceIdType.MESH


def kernel(views, shifts, out, own, mir, band, flat, rows, shift_row, bare, xx_ref, xu_ref, coh_ref, pull_ref, both_ref,
           turned, ext, facing, table, coh_chunk, pull_chunk, costs, result,
           load_sem, zsend, zrecv, psend, precv, ready, ready_all, go):
    au = lax.axis_index("au")
    vert = lax.axis_index("vert")
    other = 30 - 2 * (vert // 2) + lax.rem(vert, 2)
    first = vert < 16
    middle = jnp.logical_and(vert >= 6, vert < 26)
    flight = CAMS
    for slot, count in ((24, 3), (26, 10), (28, 8), (30, 6), (6, 8)):
        flight = jnp.where(jnp.logical_and(vert >= slot, vert < slot + 2), count, flight)

    load = pltpu.make_async_copy(views.at[0, 0], band, load_sem.at[0])
    load.start()
    load_shift = pltpu.make_async_copy(shifts.at[0], shift_row, load_sem.at[1])
    load_shift.start()

    def peer(k):
        return lax.rem(au + k, CAMS)

    def signal(sem, column, slot):
        pl.semaphore_signal(sem, inc=1, device_id={"au": column, "vert": slot}, device_id_type=MESH)

    def each(low, high, fn, unroll=None):
        def body(k, _):
            fn(k)
            return 0

        lax.fori_loop(low, high, body, 0, unroll=unroll)

    ahead_of = lax.rem(CAMS + 1 - au, CAMS)

    def across(i):
        k = jnp.where(i == 0, ahead_of, jnp.where(i <= ahead_of, i - 1, i))
        return pltpu.make_async_remote_copy(
            src_ref=rows.at[peer(k), pl.ds(0, TILES)],
            dst_ref=mir.at[k],
            send_sem=zsend.at[k],
            recv_sem=zrecv.at[k],
            device_id={"au": peer(k), "vert": other},
            device_id_type=MESH,
        )

    def arrival(k):
        return pltpu.make_async_remote_copy(
            src_ref=rows.at[au, pl.ds(0, TILES)],
            dst_ref=mir.at[k],
            send_sem=zsend.at[k],
            recv_sem=zrecv.at[k],
            device_id={"au": au, "vert": other},
            device_id_type=MESH,
        )

    def inside(k):
        return pltpu.make_async_remote_copy(
            src_ref=rows.at[peer(k)],
            dst_ref=own.at[au],
            send_sem=psend.at[k],
            recv_sem=precv.at[k],
            device_id={"au": peer(k), "vert": vert},
            device_id_type=MESH,
        )

    def rest(k):
        across(k - flight).wait_send()
        across(k).start()

    barrier = pltpu.get_barrier_semaphore()

    @pl.when(jnp.logical_or(first, middle))
    def _():
        for k in range(1, CAMS):
            signal(barrier, peer(k), vert)

    load.wait()
    for t in range(TILES):
        flat[pl.ds(t, ROWS, stride=TILES), :] = band[:, t * LANES : (t + 1) * LANES].astype(jnp.float32)
    for y in range(ROWS):
        rows[y, 0:TILES, :] = flat[y * TILES : (y + 1) * TILES, :].astype(jnp.bfloat16)

    def fill():
        load_shift.wait()
        labels = jnp.concatenate([shift_row[...].astype(jnp.float32), jnp.zeros((1, LANES - 32), jnp.float32)], axis=1)
        labels = jnp.broadcast_to(labels, (16, LANES)).astype(jnp.bfloat16)
        for y in range(ROWS):
            rows[y, TILES : TILES + 16, :] = labels

    @pl.when(first)
    def _():
        pl.semaphore_wait(barrier, CAMS - 1)
        signal(barrier, au, other)
        fill()
        each(1, CAMS, lambda k: inside(k).start())
        pl.semaphore_wait(ready, 1)

        @pl.when(jnp.logical_not(middle))
        def _():
            for k in range(1, CAMS):
                signal(ready_all, peer(k), vert)
            pl.semaphore_wait(ready_all, CAMS - 1)
            signal(go, au, other)

        each(0, flight, lambda k: across(k).start())

    @pl.when(jnp.logical_not(first))
    def _():
        @pl.when(middle)
        def _():
            pl.semaphore_wait(barrier, CAMS)

        @pl.when(jnp.logical_not(middle))
        def _():
            pl.semaphore_wait(barrier, 1)

        signal(ready, au, other)
        each(0, flight, lambda k: across(k).start())
        fill()

        @pl.when(jnp.logical_not(middle))
        def _():
            pl.semaphore_wait(go, 1)

        each(1, CAMS, lambda k: inside(k).start())

        each(flight, CAMS, rest)

    keep = pltpu.make_async_copy(rows.at[au], own.at[au], load_sem.at[2])
    keep.start()
    keep.wait()
    each(1, CAMS, lambda k: inside(k).wait_recv())

    blank = jnp.zeros((TILES, LANES), jnp.float32)
    wide_lane = lax.broadcasted_iota(jnp.int32, (TILES, LANES), 1)
    wide_tile = lax.broadcasted_iota(jnp.int32, (TILES, LANES), 0)

    def ahead(value, d):
        a = pltpu.roll(value, LANES - d, 1)
        b = jnp.where(wide_tile == TILES - 1, blank, pltpu.roll(a, TILES - 1, 0))
        return jnp.where(wide_lane >= LANES - d, b, a)

    def behind(value, d):
        a = pltpu.roll(value, d, 1)
        b = jnp.where(wide_tile == 0, blank, pltpu.roll(a, 1, 0))
        return jnp.where(wide_lane < d, b, a)

    def at(a):
        return pl.ds(pl.multiple_of((a + 1) * TILES, TILES), TILES)

    for ref in (bare, xx_ref, xu_ref):
        ref[0:TILES, :] = blank
        ref[(CAMS + 1) * TILES : (CAMS + 2) * TILES, :] = blank
    bare[TILES : (CAMS + 1) * TILES, :] = own[:, 0:TILES, :].astype(jnp.float32).reshape(CAMS * TILES, LANES)

    def gradients(a):
        value = bare[at(a), :]
        gx = ahead(value, 1) - behind(value, 1)
        gu = bare[at(a + 1), :] - bare[at(a - 1), :]
        xx_ref[at(a), :] = gx * gx
        xu_ref[at(a), :] = gx * gu

    each(0, CAMS, gradients, 4)

    def boxes(a):
        def box(ref):
            value = ref[at(a - 1), :] + ref[at(a), :] + ref[at(a + 1), :]
            return (behind(value, 2) + behind(value, 1) + value + ahead(value, 1) + ahead(value, 2)) * 0.25

        jxx, jxu = box(xx_ref), box(xu_ref)
        inv = 1.0 / (jxx + 1.0)
        coh = jxx * inv
        coh_ref[at(a - 1), :] = coh
        pull_ref[at(a - 1), :] = 4.0 * coh * (-jxu * inv)

    each(0, CAMS, boxes, 4)

    shift = own[:, TILES, :].astype(jnp.float32)
    offset = lax.broadcasted_iota(jnp.int32, (CAMS, LANES), 1).astype(jnp.float32) - MAXS
    often = jnp.zeros((CAMS, LANES), jnp.float32)
    total = jnp.zeros((CAMS, LANES), jnp.float32)
    for label in range(32):
        hit = shift[:, label : label + 1] == offset
        often = often + jnp.where(hit, 1.0, 0.0)
        total = total + jnp.where(hit, float(label), 0.0)
    both_ref[...] = often + pltpu.roll(total, 64, 1)

    lane = lax.broadcasted_iota(jnp.int32, (8, LANES), 1)
    sub = lax.broadcasted_iota(jnp.int32, (8, LANES), 0)
    first_tile, last_tile = lane % 32 == 0, lane % 32 == TILES - 1
    zero = jnp.zeros((8, LANES), jnp.float32)

    def right_of(value):
        a = pltpu.roll(value, 7, 0)
        b = jnp.where(last_tile, zero, pltpu.roll(a, LANES - 1, 1))
        return jnp.where(sub == 7, b, a)

    def left_of(value):
        a = pltpu.roll(value, 1, 0)
        b = jnp.where(first_tile, zero, pltpu.roll(a, 1, 1))
        return jnp.where(sub == 0, b, a)

    def camera(g, j):
        return lax.rem(2 * CAMS - 1 - au + 4 * g + j, CAMS)

    def put(ref, start, i, value):
        ref[pl.ds(pl.multiple_of((start + i) * 8, 8), 8), :] = value

    def get(ref, start, i):
        return ref[pl.ds(pl.multiple_of((start + i) * 8, 8), 8), :]

    def extend(block, ref, start):
        turned[...] = (block * SCALE).T
        values = [turned[pl.ds(i, 8, stride=SEG), :] for i in range(SEG)]
        right = [right_of(v) for v in values]
        right += [right_of(v) for v in right[:RAD]]
        left = [left_of(v) for v in values]
        left = [left_of(v) for v in left[-RAD:]] + left
        for i, value in enumerate(left + values + right):
            put(ref, start, i, value)

    def prepare(g):
        cams = [camera(g, j) for j in range(4)]

        def natural(ref):
            return jnp.concatenate([ref[pl.ds(pl.multiple_of(c * TILES, TILES), TILES), :] for c in cams], axis=0)

        block = jnp.concatenate([bare[at(c), :] for c in cams], axis=0)
        extend(block, ext, g * EXT)
        here = pl.ds(pl.multiple_of(g * LANES, LANES), LANES)
        coh_chunk[here, :] = natural(coh_ref).T
        pull_chunk[here, :] = natural(pull_ref).T
        labels = [jnp.broadcast_to(both_ref[pl.ds(c, 1), :], (TILES, LANES)) for c in cams]
        table[here, :] = jnp.concatenate(labels, axis=0).T

    each(0, 4, prepare)

    @pl.when(first)
    def _():
        each(flight, CAMS, rest)

    outside_left = jnp.where(jnp.logical_and(first_tile, sub == 0), 0.0, 1.0)
    outside_right = jnp.where(jnp.logical_and(last_tile, sub == 7), 0.0, 1.0)

    def boxed(values):
        sums = []
        for i in range(len(values) - 4):
            if i % 8 == 0:
                sums.append((values[i] + values[i + 1]) + (values[i + 2] + values[i + 3]) + values[i + 4])
            else:
                sums.append(sums[-1] + (values[i + 4] - values[i - 1]))
        return sums

    def chunk(g):
        each(0, 4, lambda j: arrival(4 * g + j).wait_recv())

        extend(mir[pl.ds(4 * g, 4), :, :].astype(jnp.float32).reshape(LANES, LANES), facing, 0)

        def entry(s):
            return jnp.broadcast_to(table[pl.ds(g * LANES + s, 1), :], (8, LANES))

        best = [zero + FAR for _ in range(SEG)]
        for s in range(OFFS):
            step = s - MAXS
            squares = []
            for i in range(SEG + 2 * RAD):
                d = get(ext, g * EXT, HALO - RAD + i + step) - get(facing, 0, HALO - RAD + i - step)
                squares.append(d * d)
            squares[:RAD] = [q * outside_left for q in squares[:RAD]]
            squares[-RAD:] = [q * outside_right for q in squares[-RAD:]]
            miss = jnp.where(entry(s) > 0.0, 0.0, FAR)
            for i, cost in enumerate(boxed(squares)):
                cost = cost + miss
                put(costs, s * SEG, i, cost)
                best[i] = jnp.minimum(best[i], cost)
        den = [zero for _ in range(SEG)]
        num = [zero for _ in range(SEG)]
        for s in range(OFFS):
            n, m = entry(s), entry(64 + s)
            for i in range(SEG):
                e = jnp.exp2(best[i] - get(costs, s * SEG, i))
                den[i] = den[i] + e * n
                num[i] = num[i] + e * m
        for i in range(SEG):
            here = pl.ds(g * LANES + i, 8, stride=SEG)
            conf = 1.0 / den[i]
            depth = num[i] * conf
            value = (conf * depth + pull_chunk[here, :]) / (conf + coh_chunk[here, :])
            result[pl.ds(i, 8, stride=SEG), :] = value
        back = result[...].T
        for j in range(4):
            out[camera(g, j)] = back[j * TILES : (j + 1) * TILES]

    each(0, 4, chunk)

    each(CAMS - flight, CAMS, lambda k: across(k).wait_send())
    each(1, CAMS, lambda k: inside(k).wait_send())


def local(views, shifts):
    f32, bf16 = jnp.float32, jnp.bfloat16
    dma = pltpu.SemaphoreType.DMA
    out = pl.pallas_call(
        kernel,
        out_shape=jax.ShapeDtypeStruct((CAMS, TILES, LANES), f32),
        in_specs=[pl.BlockSpec(memory_space=pltpu.HBM)] * 2,
        out_specs=pl.BlockSpec(memory_space=pltpu.VMEM),
        scratch_shapes=[
            pltpu.VMEM((CAMS, TILES + 16, LANES), bf16),
            pltpu.VMEM((CAMS, TILES, LANES), bf16),
            pltpu.VMEM((ROWS, TILES * LANES), bf16),
            pltpu.VMEM((ROWS * TILES, LANES), f32),
            pltpu.VMEM((ROWS, TILES + 16, LANES), bf16),
            pltpu.VMEM((1, 32), jnp.int32),
            pltpu.VMEM(((CAMS + 2) * TILES, LANES), f32),
            pltpu.VMEM(((CAMS + 2) * TILES, LANES), f32),
            pltpu.VMEM(((CAMS + 2) * TILES, LANES), f32),
            pltpu.VMEM((CAMS * TILES, LANES), f32),
            pltpu.VMEM((CAMS * TILES, LANES), f32),
            pltpu.VMEM((CAMS, LANES), f32),
            pltpu.VMEM((LANES, LANES), f32),
            pltpu.VMEM((4 * EXT * 8, LANES), f32),
            pltpu.VMEM((EXT * 8, LANES), f32),
            pltpu.VMEM((4 * LANES, LANES), f32),
            pltpu.VMEM((4 * LANES + SEG, LANES), f32),
            pltpu.VMEM((4 * LANES + SEG, LANES), f32),
            pltpu.VMEM((OFFS * SEG * 8, LANES), f32),
            pltpu.VMEM((LANES, LANES), f32),
            dma((3,)),
            dma((CAMS,)),
            dma((CAMS,)),
            dma((CAMS,)),
            dma((CAMS,)),
            pltpu.SemaphoreType.REGULAR,
            pltpu.SemaphoreType.REGULAR,
            pltpu.SemaphoreType.REGULAR,
        ],
        compiler_params=pltpu.CompilerParams(
            collective_id=0, has_side_effects=True, vmem_limit_bytes=32 * 1024 * 1024
        ),
        name="light_field",
    )(*[pltpu.with_memory_space_constraint(a, pltpu.HBM) for a in (views, shifts)])
    return out.reshape(1, CAMS, 1, TILES * LANES)


def solution(mesh):
    placed = (P("vert", "au", None, None), P("vert", "au", None))
    return jax.shard_map(
        local, mesh=mesh, in_specs=placed, out_specs=P("vert", None, "au", None), check_vma=False
    )
```

```python
import functools
import math

import jax
import jax.numpy as jnp
from jax import lax
from jax.experimental import pallas as pl
from jax.experimental.pallas import tpu as pltpu
from jax.sharding import PartitionSpec as P

MAXS = 16
RAD = 2
OFFS = 2 * MAXS + 1
CAMS = 16
ROWS = 16
TILES = 32
LANES = 128
SEG = 16
HALO = MAXS + RAD
EXT = SEG + 2 * HALO
SCALE = math.sqrt(0.5 * math.log2(math.e))
FAR = 1e30
MESH = pl.DeviceIdType.MESH


def kernel(views, shifts, out, own, mir, band, flat, rows, shift_row, bare, xx_ref, xu_ref, coh_ref, pull_ref, both_ref,
           turned, ext, facing, table, coh_chunk, pull_chunk, costs, result,
           load_sem, zsend, zrecv, psend, precv, ready, ready_all, go):
    au = lax.axis_index("au")
    vert = lax.axis_index("vert")
    other = 30 - 2 * (vert // 2) + lax.rem(vert, 2)
    first = vert < 16
    middle = jnp.logical_and(vert >= 6, vert < 26)
    flight = CAMS
    for slot, count in ((24, 3), (26, 10), (28, 8), (30, 6), (6, 8), (4, 8)):
        flight = jnp.where(jnp.logical_and(vert >= slot, vert < slot + 2), count, flight)

    load = pltpu.make_async_copy(views.at[0, 0], band, load_sem.at[0])
    load.start()
    load_shift = pltpu.make_async_copy(shifts.at[0], shift_row, load_sem.at[1])
    load_shift.start()

    def peer(k):
        return lax.rem(au + k, CAMS)

    def signal(sem, column, slot):
        pl.semaphore_signal(sem, inc=1, device_id={"au": column, "vert": slot}, device_id_type=MESH)

    def each(low, high, fn, unroll=None):
        def body(k, _):
            fn(k)
            return 0

        lax.fori_loop(low, high, body, 0, unroll=unroll)

    ahead_of = lax.rem(CAMS + 1 - au, CAMS)

    def across(i):
        k = jnp.where(i == 0, ahead_of, jnp.where(i <= ahead_of, i - 1, i))
        return pltpu.make_async_remote_copy(
            src_ref=rows.at[peer(k), pl.ds(0, TILES)],
            dst_ref=mir.at[k],
            send_sem=zsend.at[k],
            recv_sem=zrecv.at[k],
            device_id={"au": peer(k), "vert": other},
            device_id_type=MESH,
        )

    def arrival(k):
        return pltpu.make_async_remote_copy(
            src_ref=rows.at[au, pl.ds(0, TILES)],
            dst_ref=mir.at[k],
            send_sem=zsend.at[k],
            recv_sem=zrecv.at[k],
            device_id={"au": au, "vert": other},
            device_id_type=MESH,
        )

    def inside(k):
        return pltpu.make_async_remote_copy(
            src_ref=rows.at[peer(k)],
            dst_ref=own.at[au],
            send_sem=psend.at[k],
            recv_sem=precv.at[k],
            device_id={"au": peer(k), "vert": vert},
            device_id_type=MESH,
        )

    def rest(k):
        across(k - flight).wait_send()
        across(k).start()

    barrier = pltpu.get_barrier_semaphore()

    @pl.when(jnp.logical_or(first, middle))
    def _():
        for k in range(1, CAMS):
            signal(barrier, peer(k), vert)

    load.wait()
    for t in range(TILES):
        flat[pl.ds(t, ROWS, stride=TILES), :] = band[:, t * LANES : (t + 1) * LANES].astype(jnp.float32)
    for y in range(ROWS):
        rows[y, 0:TILES, :] = flat[y * TILES : (y + 1) * TILES, :].astype(jnp.bfloat16)

    def fill():
        load_shift.wait()
        labels = jnp.concatenate([shift_row[...].astype(jnp.float32), jnp.zeros((1, LANES - 32), jnp.float32)], axis=1)
        labels = jnp.broadcast_to(labels, (16, LANES)).astype(jnp.bfloat16)
        for y in range(ROWS):
            rows[y, TILES : TILES + 16, :] = labels

    @pl.when(first)
    def _():
        pl.semaphore_wait(barrier, CAMS - 1)
        signal(barrier, au, other)
        fill()
        each(1, CAMS, lambda k: inside(k).start())
        pl.semaphore_wait(ready, 1)

        @pl.when(jnp.logical_not(middle))
        def _():
            for k in range(1, CAMS):
                signal(ready_all, peer(k), vert)
            pl.semaphore_wait(ready_all, CAMS - 1)
            signal(go, au, other)

        each(0, flight, lambda k: across(k).start())

    @pl.when(jnp.logical_not(first))
    def _():
        @pl.when(middle)
        def _():
            pl.semaphore_wait(barrier, CAMS)

        @pl.when(jnp.logical_not(middle))
        def _():
            pl.semaphore_wait(barrier, 1)

        signal(ready, au, other)
        each(0, flight, lambda k: across(k).start())
        fill()

        @pl.when(jnp.logical_not(middle))
        def _():
            pl.semaphore_wait(go, 1)

        each(1, CAMS, lambda k: inside(k).start())

        each(flight, CAMS, rest)

    keep = pltpu.make_async_copy(rows.at[au], own.at[au], load_sem.at[2])
    keep.start()
    keep.wait()
    each(1, CAMS, lambda k: inside(k).wait_recv())

    blank = jnp.zeros((TILES, LANES), jnp.float32)
    wide_lane = lax.broadcasted_iota(jnp.int32, (TILES, LANES), 1)
    wide_tile = lax.broadcasted_iota(jnp.int32, (TILES, LANES), 0)

    def ahead(value, d):
        a = pltpu.roll(value, LANES - d, 1)
        b = jnp.where(wide_tile == TILES - 1, blank, pltpu.roll(a, TILES - 1, 0))
        return jnp.where(wide_lane >= LANES - d, b, a)

    def behind(value, d):
        a = pltpu.roll(value, d, 1)
        b = jnp.where(wide_tile == 0, blank, pltpu.roll(a, 1, 0))
        return jnp.where(wide_lane < d, b, a)

    def at(a):
        return pl.ds(pl.multiple_of((a + 1) * TILES, TILES), TILES)

    for ref in (bare, xx_ref, xu_ref):
        ref[0:TILES, :] = blank
        ref[(CAMS + 1) * TILES : (CAMS + 2) * TILES, :] = blank
    bare[TILES : (CAMS + 1) * TILES, :] = own[:, 0:TILES, :].astype(jnp.float32).reshape(CAMS * TILES, LANES)

    def gradients(a):
        value = bare[at(a), :]
        gx = ahead(value, 1) - behind(value, 1)
        gu = bare[at(a + 1), :] - bare[at(a - 1), :]
        xx_ref[at(a), :] = gx * gx
        xu_ref[at(a), :] = gx * gu

    each(0, CAMS, gradients, 4)

    def boxes(a):
        def box(ref):
            value = ref[at(a - 1), :] + ref[at(a), :] + ref[at(a + 1), :]
            return (behind(value, 2) + behind(value, 1) + value + ahead(value, 1) + ahead(value, 2)) * 0.25

        jxx, jxu = box(xx_ref), box(xu_ref)
        inv = 1.0 / (jxx + 1.0)
        coh = jxx * inv
        coh_ref[at(a - 1), :] = coh
        pull_ref[at(a - 1), :] = 4.0 * coh * (-jxu * inv)

    each(0, CAMS, boxes, 4)

    shift = own[:, TILES, :].astype(jnp.float32)
    offset = lax.broadcasted_iota(jnp.int32, (CAMS, LANES), 1).astype(jnp.float32) - MAXS
    often = jnp.zeros((CAMS, LANES), jnp.float32)
    total = jnp.zeros((CAMS, LANES), jnp.float32)
    for label in range(32):
        hit = shift[:, label : label + 1] == offset
        often = often + jnp.where(hit, 1.0, 0.0)
        total = total + jnp.where(hit, float(label), 0.0)
    both_ref[...] = often + pltpu.roll(total, 64, 1)

    lane = lax.broadcasted_iota(jnp.int32, (8, LANES), 1)
    sub = lax.broadcasted_iota(jnp.int32, (8, LANES), 0)
    first_tile, last_tile = lane % 32 == 0, lane % 32 == TILES - 1
    zero = jnp.zeros((8, LANES), jnp.float32)

    def right_of(value):
        a = pltpu.roll(value, 7, 0)
        b = jnp.where(last_tile, zero, pltpu.roll(a, LANES - 1, 1))
        return jnp.where(sub == 7, b, a)

    def left_of(value):
        a = pltpu.roll(value, 1, 0)
        b = jnp.where(first_tile, zero, pltpu.roll(a, 1, 1))
        return jnp.where(sub == 0, b, a)

    def camera(g, j):
        return lax.rem(2 * CAMS - 1 - au + 4 * g + j, CAMS)

    def put(ref, start, i, value):
        ref[pl.ds(pl.multiple_of((start + i) * 8, 8), 8), :] = value

    def get(ref, start, i):
        return ref[pl.ds(pl.multiple_of((start + i) * 8, 8), 8), :]

    def extend(block, ref, start):
        turned[...] = (block * SCALE).T
        values = [turned[pl.ds(i, 8, stride=SEG), :] for i in range(SEG)]
        right = [right_of(v) for v in values]
        right += [right_of(v) for v in right[:RAD]]
        left = [left_of(v) for v in values]
        left = [left_of(v) for v in left[-RAD:]] + left
        for i, value in enumerate(left + values + right):
            put(ref, start, i, value)

    def prepare(g):
        cams = [camera(g, j) for j in range(4)]

        def natural(ref):
            return jnp.concatenate([ref[pl.ds(pl.multiple_of(c * TILES, TILES), TILES), :] for c in cams], axis=0)

        block = jnp.concatenate([bare[at(c), :] for c in cams], axis=0)
        extend(block, ext, g * EXT)
        here = pl.ds(pl.multiple_of(g * LANES, LANES), LANES)
        coh_chunk[here, :] = natural(coh_ref).T
        pull_chunk[here, :] = natural(pull_ref).T
        labels = [jnp.broadcast_to(both_ref[pl.ds(c, 1), :], (TILES, LANES)) for c in cams]
        table[here, :] = jnp.concatenate(labels, axis=0).T

    each(0, 4, prepare)

    @pl.when(first)
    def _():
        each(flight, CAMS, rest)

    outside_left = jnp.where(jnp.logical_and(first_tile, sub == 0), 0.0, 1.0)
    outside_right = jnp.where(jnp.logical_and(last_tile, sub == 7), 0.0, 1.0)

    def boxed(values):
        sums = []
        for i in range(len(values) - 4):
            if i % 8 == 0:
                sums.append((values[i] + values[i + 1]) + (values[i + 2] + values[i + 3]) + values[i + 4])
            else:
                sums.append(sums[-1] + (values[i + 4] - values[i - 1]))
        return sums

    def chunk(g):
        each(0, 4, lambda j: arrival(4 * g + j).wait_recv())

        extend(mir[pl.ds(4 * g, 4), :, :].astype(jnp.float32).reshape(LANES, LANES), facing, 0)

        def entry(s):
            return jnp.broadcast_to(table[pl.ds(g * LANES + s, 1), :], (8, LANES))

        best = [zero + FAR for _ in range(SEG)]
        for s in range(OFFS):
            step = s - MAXS
            squares = []
            for i in range(SEG + 2 * RAD):
                d = get(ext, g * EXT, HALO - RAD + i + step) - get(facing, 0, HALO - RAD + i - step)
                squares.append(d * d)
            squares[:RAD] = [q * outside_left for q in squares[:RAD]]
            squares[-RAD:] = [q * outside_right for q in squares[-RAD:]]
            miss = jnp.where(entry(s) > 0.0, 0.0, FAR)
            for i, cost in enumerate(boxed(squares)):
                cost = cost + miss
                put(costs, s * SEG, i, cost)
                best[i] = jnp.minimum(best[i], cost)
        den = [zero for _ in range(SEG)]
        num = [zero for _ in range(SEG)]
        for s in range(OFFS):
            n, m = entry(s), entry(64 + s)
            for i in range(SEG):
                e = jnp.exp2(best[i] - get(costs, s * SEG, i))
                den[i] = den[i] + e * n
                num[i] = num[i] + e * m
        for i in range(SEG):
            here = pl.ds(g * LANES + i, 8, stride=SEG)
            conf = 1.0 / den[i]
            depth = num[i] * conf
            value = (conf * depth + pull_chunk[here, :]) / (conf + coh_chunk[here, :])
            result[pl.ds(i, 8, stride=SEG), :] = value
        back = result[...].T
        for j in range(4):
            out[camera(g, j)] = back[j * TILES : (j + 1) * TILES]

    each(0, 4, chunk)

    each(CAMS - flight, CAMS, lambda k: across(k).wait_send())
    each(1, CAMS, lambda k: inside(k).wait_send())


def local(views, shifts):
    f32, bf16 = jnp.float32, jnp.bfloat16
    dma = pltpu.SemaphoreType.DMA
    out = pl.pallas_call(
        kernel,
        out_shape=jax.ShapeDtypeStruct((CAMS, TILES, LANES), f32),
        in_specs=[pl.BlockSpec(memory_space=pltpu.HBM)] * 2,
        out_specs=pl.BlockSpec(memory_space=pltpu.VMEM),
        scratch_shapes=[
            pltpu.VMEM((CAMS, TILES + 16, LANES), bf16),
            pltpu.VMEM((CAMS, TILES, LANES), bf16),
            pltpu.VMEM((ROWS, TILES * LANES), bf16),
            pltpu.VMEM((ROWS * TILES, LANES), f32),
            pltpu.VMEM((ROWS, TILES + 16, LANES), bf16),
            pltpu.VMEM((1, 32), jnp.int32),
            pltpu.VMEM(((CAMS + 2) * TILES, LANES), f32),
            pltpu.VMEM(((CAMS + 2) * TILES, LANES), f32),
            pltpu.VMEM(((CAMS + 2) * TILES, LANES), f32),
            pltpu.VMEM((CAMS * TILES, LANES), f32),
            pltpu.VMEM((CAMS * TILES, LANES), f32),
            pltpu.VMEM((CAMS, LANES), f32),
            pltpu.VMEM((LANES, LANES), f32),
            pltpu.VMEM((4 * EXT * 8, LANES), f32),
            pltpu.VMEM((EXT * 8, LANES), f32),
            pltpu.VMEM((4 * LANES, LANES), f32),
            pltpu.VMEM((4 * LANES + SEG, LANES), f32),
            pltpu.VMEM((4 * LANES + SEG, LANES), f32),
            pltpu.VMEM((OFFS * SEG * 8, LANES), f32),
            pltpu.VMEM((LANES, LANES), f32),
            dma((3,)),
            dma((CAMS,)),
            dma((CAMS,)),
            dma((CAMS,)),
            dma((CAMS,)),
            pltpu.SemaphoreType.REGULAR,
            pltpu.SemaphoreType.REGULAR,
            pltpu.SemaphoreType.REGULAR,
        ],
        compiler_params=pltpu.CompilerParams(
            collective_id=0, has_side_effects=True, vmem_limit_bytes=32 * 1024 * 1024
        ),
        name="light_field",
    )(*[pltpu.with_memory_space_constraint(a, pltpu.HBM) for a in (views, shifts)])
    return out.reshape(1, CAMS, 1, TILES * LANES)


def solution(mesh):
    placed = (P("vert", "au", None, None), P("vert", "au", None))
    return jax.shard_map(
        local, mesh=mesh, in_specs=placed, out_specs=P("vert", None, "au", None), check_vma=False
    )
```
